512 devices in a mesh: dp: 512 (over z, y, x, core).
Axes of the slice: x: 4, y: 4, z: 16, core: 2. Of those that a mesh axis runs over, the one named last changes fastest.
Arguments:
- picture_vectors: bfloat16 [131072, 1152], P('dp'), may hold values from -0.19921875 to 0.19921875
- caption_vectors: bfloat16 [131072, 1152], P('dp'), may hold values from -0.19921875 to 0.19921875
- sharpness_factor: float32 [1], replicated, may hold values from 4 to 12
- affinity_offset: float32 [1], replicated, may hold values from -3 to -1
Outputs:
- loss_rows: float32 [131072], P('dp')
- image_embedding_gradient: float32 [131072, 1152], P('dp')
- text_grad: float32 [131072, 1152], P('dp')
The draws below stay inside these ranges and needn't reach their ends.
All inputs are finite; a program needn't handle non-finite values.
Results may differ from the reference program's by a relative error of at most 0.0043.
Values may be sent and summed in bfloat16 or wider, within the bound.
A program may use at most 64 MiB of HBM per device.

```python
import jax
import jax.numpy as jnp
from jax import lax

D = 1152
ROWS = 256
STEPS = 8
TOKENS = 131072
N_DP = 512


def steps_of(key, shape, pieces, least, largest):
    def one(position, parts):
        heights = jax.random.uniform(jax.random.fold_in(jax.random.fold_in(key, 6), position), (parts,), jnp.float32, least / len(pieces), largest / len(pieces))
        return jnp.repeat(jnp.exp(heights), shape[position] // parts).reshape((-1,) + (1,) * (len(shape) - position - 1))

    gain = one(*pieces[0])
    for cut in pieces[1:]:
        gain = gain * one(*cut)
    return gain


def gaussian(rng, shape, scale, limit, shards=(), kind=jnp.bfloat16):
    result = scale * jax.random.normal(rng, shape, jnp.float32)
    if shards:
        result = result * steps_of(rng, shape, shards, -0.22, 0.18)
    return jnp.clip(result, -limit, limit).astype(kind)


def setup_inputs(seed: int = 0) -> dict:
    streams_of = jax.random.split(jax.random.key(seed), 5)
    return {
        "picture_vectors": gaussian(streams_of[0], (TOKENS, D), 0.03, 0.19921875, ((0, 512),)),
        "caption_vectors": gaussian(streams_of[1], (TOKENS, D), 0.03, 0.19921875, ((0, 512),)),
        "sharpness_factor": jnp.clip(jax.random.uniform(streams_of[2], (1,), jnp.float32, 4.0, 12.0), 4.0, 12.0),
        "affinity_offset": jnp.clip(jax.random.uniform(streams_of[3], (1,), jnp.float32, -3.0, -1.0), -3.0, -1.0),
    }


def normed(values):
    full = values.astype(jnp.float32)
    length = jnp.sqrt(lax.optimization_barrier(jnp.sum(full * full, axis=1, keepdims=True)) + 1e-06)
    return (full / length, length)

def reference(picture_vectors, caption_vectors, sharpness_factor, affinity_offset):
    img_unit, image_norm_values = normed(picture_vectors)
    txt_unit, text_norm_values = normed(caption_vectors)
    image_widened = lax.optimization_barrier(img_unit.astype(jnp.bfloat16)).astype(jnp.float32)
    txt_wide = lax.optimization_barrier(txt_unit.astype(jnp.bfloat16)).astype(jnp.float32)
    img_blocks = image_widened.reshape(N_DP, ROWS, D)
    txt_blocks = txt_wide.reshape(N_DP, ROWS, D)
    similarity_multiplier = sharpness_factor[0]
    offset = affinity_offset[0]
    diagonal = jnp.eye(ROWS, dtype=bool)
    loss_sum = jnp.zeros((N_DP, ROWS), jnp.float32)
    image_normalized = jnp.zeros((N_DP, ROWS, D), jnp.float32)
    txt_hat = jnp.zeros((N_DP, ROWS, D), jnp.float32)
    for step in range(STEPS):
        matched_counterpart = jnp.roll(txt_blocks, step, axis=0)
        similarity_matrix = jnp.einsum('nrd,nsd->nrs', img_blocks, matched_counterpart)
        logits = similarity_multiplier * similarity_matrix + offset
        if step == 0:
            label = jnp.where(diagonal, 1.0, -1.0).astype(jnp.float32)
        else:
            label = jnp.full((ROWS, ROWS), -1.0, jnp.float32)
        loss_sum = loss_sum + lax.optimization_barrier(jnp.sum(jax.nn.softplus(-label * logits), axis=2))
        slope = -label * jax.nn.sigmoid(-label * logits)
        slope = lax.optimization_barrier(slope.astype(jnp.bfloat16)).astype(jnp.float32)
        image_normalized = image_normalized + similarity_multiplier * jnp.einsum('nrs,nsd->nrd', slope, matched_counterpart)
        piece = similarity_multiplier * jnp.einsum('nrs,nrd->nsd', slope, img_blocks)
        txt_hat = txt_hat + jnp.roll(piece, -step, axis=0)
    image_normalized = image_normalized.reshape(N_DP * ROWS, D)
    txt_hat = txt_hat.reshape(N_DP * ROWS, D)
    loss_rows = loss_sum.reshape(N_DP * ROWS) / (STEPS * ROWS)
    image_embedding_gradient = (image_normalized - img_unit * lax.optimization_barrier(jnp.sum(img_unit * image_normalized, axis=1, keepdims=True))) / image_norm_values
    text_grad = (txt_hat - txt_unit * lax.optimization_barrier(jnp.sum(txt_unit * txt_hat, axis=1, keepdims=True))) / text_norm_values
    return (loss_rows, image_embedding_gradient, text_grad)
```

```python
import functools

import jax
import jax.numpy as jnp
from jax import lax
from jax.experimental import pallas as pl
from jax.experimental.pallas import tpu as pltpu
from jax.sharding import PartitionSpec as P

STAGES = 4
CHUNKS = 2
LANES = 384
STRIP = 32
MESH = pl.DeviceIdType.MESH


def kernel(s_ref, b_ref, img_ref, txt_ref, loss_ref, gi_ref, gt_ref,
           own, buf, hat, losses, chain_s, chain_r, side_s, side_r):
    rows, depth = img_ref.shape
    part = rows // CHUNKS
    n = lax.axis_index("dp")
    total = lax.axis_size("dp")
    core = lax.rem(n, 2)

    def at(offset):
        return lax.rem(n + offset + total, total)

    sibling = at(1 - 2 * core)
    chain_to = (at(2), at(-2))
    first_to = (at(1 + 6 * core), at(-7 + 6 * core))
    far = at(-7 + 14 * core)

    def chain(kind, stage, chunk):
        source = buf.at[kind, stage, chunk, pl.ds(0, part)]
        return pltpu.make_async_remote_copy(
            src_ref=source,
            dst_ref=buf.at[kind, jnp.minimum(stage + 1, STAGES - 1), chunk, pl.ds(0, part)],
            send_sem=chain_s.at[kind, stage, chunk],
            recv_sem=chain_r.at[kind, stage, chunk],
            device_id=(chain_to[kind],),
            device_id_type=MESH,
        )

    def across(kind, stage, chunk, target):
        return pltpu.make_async_remote_copy(
            src_ref=buf.at[kind, stage, chunk, pl.ds(0, part)],
            dst_ref=buf.at[kind, stage, chunk, pl.ds(part, part)],
            send_sem=side_s.at[kind, stage, chunk],
            recv_sem=side_r.at[kind, stage, chunk],
            device_id=(target,),
            device_id_type=MESH,
        )

    barrier = pltpu.get_barrier_semaphore()
    for partner in (sibling, at(2), at(-2), far):
        pl.semaphore_signal(barrier, inc=1, device_id=(partner,), device_id_type=MESH)

    scale = s_ref[0]
    offset = b_ref[0]

    def normalise(kind, chunk):
        ref = (txt_ref, img_ref)[kind]
        for r in range(0, part, STRIP):
            full = ref[pl.ds(chunk * part + r, STRIP), :].astype(jnp.float32)
            length = jnp.sqrt(jnp.sum(full * full, axis=1, keepdims=True) + 1e-06)
            unit = (full * (1.0 / length)).astype(jnp.bfloat16)
            own[kind, pl.ds(chunk * part + r, STRIP), :] = unit
            buf[kind, 0, chunk, pl.ds(r, STRIP), :] = unit

    for chunk in range(CHUNKS):
        for kind in range(2):
            normalise(kind, chunk)
        if chunk == 0:
            pl.semaphore_wait(barrier, 4)
        for kind in range(2):
            chain(kind, 0, chunk).start()
            across(kind, 0, chunk, first_to[kind]).start()

    hat[...] = jnp.zeros_like(hat)
    losses[...] = jnp.zeros_like(losses)

    def unit_of(step):
        stage, chunk = step // CHUNKS, lax.rem(step, CHUNKS)
        row = lax.broadcasted_iota(jnp.int32, (rows, 2 * part), 0)
        col = lax.broadcasted_iota(jnp.int32, (rows, 2 * part), 1)
        shift = jnp.where(stage == 0, chunk * part, 2 * rows)
        same = (row == col + shift) & (col < part)
        for kind in range(2):
            across(kind, stage, chunk, sibling).wait_recv()
            scores = lax.dot_general(
                own[1 - kind], buf[kind, stage, chunk], (((1,), (1,)), ((), ())),
                preferred_element_type=jnp.float32,
            )
            logits = scale * scores + offset
            logits = jnp.where(same, -logits, logits)
            small = jnp.exp(-jnp.abs(logits))
            share = 1.0 / (1.0 + small)
            sig = jnp.where(logits >= 0, share, small * share)
            if kind == 0:
                losses[...] += jnp.maximum(logits, 0.0) + jnp.log1p(small)
            slope = jnp.where(same, -sig, sig).astype(jnp.bfloat16)
            for lane in range(0, depth, LANES):
                hat[1 - kind, :, pl.ds(lane, LANES)] += jnp.dot(
                    slope, buf[kind, stage, chunk, :, pl.ds(lane, LANES)],
                    preferred_element_type=jnp.float32,
                )

    def step_body(step, carry):
        stage, chunk = step // CHUNKS, lax.rem(step, CHUNKS)

        @pl.when(stage > 0)
        def _():
            for kind in range(2):
                chain(kind, stage - 1, chunk).wait_recv()

                @pl.when(stage < STAGES - 1)
                def _():
                    chain(kind, stage, chunk).start()

                across(kind, stage, chunk, sibling).start()

        @pl.when(step > 0)
        def _():
            unit_of(step - 1)

        return carry

    lax.fori_loop(0, STAGES * CHUNKS, step_body, 0)
    unit_of(jnp.int32(STAGES * CHUNKS - 1))

    loss_ref[...] = jnp.sum(losses[...].T, axis=0, keepdims=True) * (1.0 / (2 * STAGES * rows))
    for kind, ref, out in ((0, txt_ref, gt_ref), (1, img_ref, gi_ref)):
        def finish(i, carry, kind=kind, ref=ref, out=out):
            where = pl.ds(pl.multiple_of(i * STRIP, STRIP), STRIP)
            full = ref[where, :].astype(jnp.float32)
            length = jnp.sqrt(jnp.sum(full * full, axis=1, keepdims=True) + 1e-06)
            inverse = 1.0 / length
            unit = full * inverse
            total_hat = scale * hat[kind, where, :]
            along = jnp.sum(unit * total_hat, axis=1, keepdims=True)
            out[where, :] = (total_hat - unit * along) * inverse
            return carry

        lax.fori_loop(0, rows // STRIP, finish, 0)

    def drain(step, carry):
        stage, chunk = step // CHUNKS, lax.rem(step, CHUNKS)
        for kind in range(2):
            across(kind, stage, chunk, sibling).wait_send()

            @pl.when(stage < STAGES - 1)
            def _():
                chain(kind, stage, chunk).wait_send()

        return carry

    lax.fori_loop(0, STAGES * CHUNKS, drain, 0)


def on_device(picture_vectors, caption_vectors, sharpness_factor, affinity_offset):
    rows, depth = picture_vectors.shape
    part = rows // CHUNKS
    vmem = pl.BlockSpec(memory_space=pltpu.VMEM)
    smem = pl.BlockSpec(memory_space=pltpu.SMEM)
    loss, gi, gt = pl.pallas_call(
        kernel,
        name="window_loss",
        out_shape=(
            jax.ShapeDtypeStruct((1, rows), jnp.float32),
            jax.ShapeDtypeStruct((rows, depth), jnp.float32),
            jax.ShapeDtypeStruct((rows, depth), jnp.float32),
        ),
        in_specs=[smem, smem, vmem, vmem],
        out_specs=(vmem, vmem, vmem),
        scratch_shapes=[
            pltpu.VMEM((2, rows, depth), jnp.bfloat16),
            pltpu.VMEM((2, STAGES, CHUNKS, 2 * part, depth), jnp.bfloat16),
            pltpu.VMEM((2, rows, depth), jnp.float32),
            pltpu.VMEM((rows, 2 * part), jnp.float32),
            pltpu.SemaphoreType.DMA((2, STAGES, CHUNKS)),
            pltpu.SemaphoreType.DMA((2, STAGES, CHUNKS)),
            pltpu.SemaphoreType.DMA((2, STAGES, CHUNKS)),
            pltpu.SemaphoreType.DMA((2, STAGES, CHUNKS)),
        ],
        compiler_params=pltpu.CompilerParams(
            collective_id=0, has_side_effects=True, vmem_limit_bytes=48 * 2**20
        ),
        cost_estimate=pl.CostEstimate(
            flops=32 * 2 * rows * rows * depth, bytes_accessed=12 * rows * depth, transcendentals=32 * rows * rows
        ),
    )(sharpness_factor, affinity_offset, picture_vectors, caption_vectors)
    return loss.reshape(rows), gi, gt


def solution(mesh):
    placed = (P("dp", None), P("dp", None), P(), P())
    return jax.shard_map(
        on_device,
        mesh=mesh,
        in_specs=placed,
        out_specs=(P("dp"), P("dp", None), P("dp", None)),
        check_vma=False,
    )
```

```python
import jax
import jax.numpy as jnp
from jax import lax
from jax.experimental import pallas as pl
from jax.experimental.pallas import tpu as pltpu
from jax.sharding import PartitionSpec as P

WINDOW = 8
COLUMNS = 4
CHUNKS = 2
LANES = 384
STRIP = 32
TEXT, IMAGE = 0, 1
OWN, CROSS = 0, 1
RIGHT, LEFT = 0, 1
MESH = pl.DeviceIdType.MESH


def kernel(s_ref, b_ref, img_hbm, txt_hbm, loss_ref, gi_ref, gt_ref,
           raw, source, block, hat, losses, in_sem,
           row_s, row_r, hop_s, hop_r, relay_s, relay_r, pair_s, pair_r, row_ok, far_ok):
    rows, depth = raw.shape[1:]
    part = rows // CHUNKS
    n = lax.axis_index("dp")
    total = lax.axis_size("dp")
    core = lax.rem(n, 2)
    chip = n // 2
    column = lax.rem(chip, COLUMNS)
    row = chip // COLUMNS

    def at(offset):
        return lax.rem(n + offset + total, total)

    def in_row(offset):
        return (row * COLUMNS + lax.rem(column + offset + COLUMNS, COLUMNS)) * 2

    stride = 2 * COLUMNS
    sibling = n + 1 - 2 * core
    lead = n - core

    def lead_at(offset):
        return lax.rem(lead + offset + total, total)

    loads = [
        pltpu.make_async_copy(ref, raw.at[kind], in_sem.at[kind])
        for kind, ref in ((TEXT, txt_hbm), (IMAGE, img_hbm))
    ]
    for load in loads:
        load.start()

    barrier = pltpu.get_barrier_semaphore()

    def greet(device):
        pl.semaphore_signal(barrier, inc=1, device_id=(device,), device_id_type=MESH)

    greet(in_row(1))
    greet(in_row(-1))
    greet(lead_at(-stride))
    greet(lead_at(-2))
    greet(lead_at(stride) + 1)
    greet(lead_at(2) + 1)

    @pl.when(core == 1)
    def _():
        greet(sibling)

    def rows_of(chunk):
        return pl.ds(pl.multiple_of(chunk * part, part), part)

    mine = pl.ds(0, part)
    others = pl.ds(part, part)

    def copy(src, dst, send, recv, device):
        return pltpu.make_async_remote_copy(
            src_ref=src, dst_ref=dst, send_sem=send, recv_sem=recv, device_id=(device,), device_id_type=MESH
        )

    def to_row(kind, chunk):
        target = jnp.where(kind == TEXT, at(stride), at(-stride))
        return copy(source.at[kind, OWN, rows_of(chunk)], source.at[kind, CROSS, rows_of(chunk)],
                    row_s.at[kind, chunk], row_r.at[kind, chunk], target)

    def hop(kind, way, chunk, version):
        target = jnp.where(way == RIGHT, in_row(1), in_row(-1)) + core
        return copy(source.at[kind, version, rows_of(chunk)], block.at[1 + way, kind, chunk, mine],
                    hop_s.at[way, kind, chunk], hop_r.at[way, kind, chunk], target)

    def relay(kind, chunk):
        target = jnp.where(chunk == 1, at(2), at(-2))
        return copy(block.at[2 - chunk, kind, chunk, mine], block.at[3, kind, chunk, mine],
                    relay_s.at[kind, chunk], relay_r.at[kind, chunk], target)

    def across(group, kind, chunk, src):
        return copy(src, block.at[group, kind, chunk, others],
                    pair_s.at[group, kind, chunk], pair_r.at[group, kind, chunk], sibling)

    def sends_own(kind, way):
        first, last = column == 0, column == COLUMNS - 1
        return (
            (jnp.logical_not(last), first) if kind == TEXT else (last, jnp.logical_not(first))
        )[way]

    scale = s_ref[0]
    offset = b_ref[0]

    def normalise(kind, chunk):
        for r in range(0, part, STRIP):
            where = pl.ds(chunk * part + r, STRIP)
            full = raw[kind, where, :].astype(jnp.float32)
            length = jnp.sqrt(jnp.sum(full * full, axis=1, keepdims=True) + 1e-06)
            unit = (full * (1.0 / length)).astype(jnp.bfloat16)
            source[kind, OWN, where, :] = unit
            block[0, kind, chunk, pl.ds(r, STRIP), :] = unit

    for chunk in range(CHUNKS):
        for kind in (TEXT, IMAGE):
            if chunk == 0:
                loads[kind].wait()
            normalise(kind, chunk)
        if chunk == 0:
            @pl.when(core == 0)
            def _():
                pl.semaphore_wait(barrier, 9)
                pl.semaphore_signal(row_ok, inc=1, device_id=(sibling,), device_id_type=MESH)

            @pl.when(core == 1)
            def _():
                pl.semaphore_wait(row_ok, 1)

        for kind in (TEXT, IMAGE):
            for way in (RIGHT, LEFT):
                @pl.when(sends_own(kind, way))
                def _():
                    hop(kind, way, chunk, OWN).start()

        to_row(TEXT, chunk).start()

    hat[...] = jnp.zeros_like(hat)
    losses[...] = jnp.zeros_like(losses)

    @pl.when(core == 1)
    def _():
        pl.semaphore_wait(barrier, 4)
        pl.semaphore_signal(far_ok, inc=1, device_id=(sibling,), device_id_type=MESH)

    @pl.when(core == 0)
    def _():
        pl.semaphore_wait(far_ok, 1)

    for chunk in range(CHUNKS):
        to_row(IMAGE, chunk).start()

    early = (jnp.where(column == 0, IMAGE, TEXT), jnp.where(column == COLUMNS - 1, TEXT, IMAGE))
    relayed = (jnp.where(column == 1, IMAGE, TEXT), jnp.where(column == COLUMNS - 2, TEXT, IMAGE))

    def item(step):
        quarter, place = step // 4, lax.rem(step, 4)
        side, late = lax.rem(place, 2), place // 2
        group = jnp.where(quarter == 3, 3, jnp.where(quarter == 0, 0, 1 + side))
        first = jnp.where(side == 0, early[0], early[1])
        far = jnp.where(side == 0, relayed[0], relayed[1])
        kind = jnp.where(quarter == 0, 1 - side, jnp.where(quarter == 1, first, 1 - first))
        kind = jnp.where(quarter == 3, jnp.where(late == 0, far, 1 - far), kind)
        chunk = jnp.where(quarter == 3, 1 - side, late)
        return quarter, side, group, kind, chunk

    def arrival(step):
        quarter, side, group, kind, chunk = item(step)

        @pl.when(quarter == 0)
        def _():
            to_row(kind, chunk).wait_recv()
            for way in (RIGHT, LEFT):
                owned = jnp.where(kind == TEXT, sends_own(TEXT, way), sends_own(IMAGE, way))

                @pl.when(jnp.logical_not(owned))
                def _():
                    hop(kind, way, chunk, CROSS).start()

            version = jnp.where(kind == TEXT, core, 1 - core)
            across(0, kind, chunk, source.at[kind, version, rows_of(chunk)]).start()

        @pl.when(quarter > 0)
        def _():
            @pl.when(quarter < 3)
            def _():
                hop(kind, side, chunk, OWN).wait_recv()

                @pl.when(chunk == 1 - side)
                def _():
                    relay(kind, chunk).start()

            @pl.when(quarter == 3)
            def _():
                relay(kind, chunk).wait_recv()

            across(group, kind, chunk, block.at[group, kind, chunk, mine]).start()

    def work(step):
        _, _, group, kind, chunk = item(step)
        across(group, kind, chunk, block.at[group, kind, chunk, mine]).wait_recv()
        line = lax.broadcasted_iota(jnp.int32, (rows, 2 * part), 0)
        col = lax.broadcasted_iota(jnp.int32, (rows, 2 * part), 1)
        shift = jnp.where(group == 0, chunk * part, 2 * rows)
        same = (line == col + shift) & (col < part)
        scores = lax.dot_general(
            source[1 - kind, OWN], block[group, kind, chunk], (((1,), (1,)), ((), ())),
            preferred_element_type=jnp.float32,
        )
        logits = scale * scores + offset
        logits = jnp.where(same, -logits, logits)
        small = jnp.exp(-jnp.abs(logits))
        share = 1.0 / (1.0 + small)
        sig = jnp.where(logits >= 0, share, small * share)

        @pl.when(kind == TEXT)
        def _():
            losses[...] += jnp.maximum(logits, 0.0) + jnp.log1p(small)

        slope = jnp.where(same, -sig, sig).astype(jnp.bfloat16)
        for lane in range(0, depth, LANES):
            hat[1 - kind, :, pl.ds(lane, LANES)] += jnp.dot(
                slope, block[group, kind, chunk, :, pl.ds(lane, LANES)],
                preferred_element_type=jnp.float32,
            )

    def step_body(step, carry):
        @pl.when(step < 16)
        def _():
            arrival(step)

        @pl.when(step > 0)
        def _():
            work(step - 1)

        return carry

    lax.fori_loop(0, 17, step_body, 0)

    loss_ref[...] = jnp.sum(losses[...].T, axis=0, keepdims=True) * (1.0 / (WINDOW * rows))
    for kind, out in ((TEXT, gt_ref), (IMAGE, gi_ref)):
        def finish(i, carry, kind=kind, out=out):
            where = pl.ds(pl.multiple_of(i * STRIP, STRIP), STRIP)
            full = raw[kind, where, :].astype(jnp.float32)
            length = jnp.sqrt(jnp.sum(full * full, axis=1, keepdims=True) + 1e-06)
            inverse = 1.0 / length
            unit = full * inverse
            total_hat = scale * hat[kind, where, :]
            along = jnp.sum(unit * total_hat, axis=1, keepdims=True)
            out[where, :] = (total_hat - unit * along) * inverse
            return carry

        lax.fori_loop(0, rows // STRIP, finish, 0)

    def drain(step, carry):
        kind, chunk = step // CHUNKS, lax.rem(step, CHUNKS)
        to_row(kind, chunk).wait_send()
        for way in (RIGHT, LEFT):
            hop(kind, way, chunk, OWN).wait_send()
        relay(kind, chunk).wait_send()
        for group in range(4):
            across(group, kind, chunk, block.at[group, kind, chunk, mine]).wait_send()
        return carry

    lax.fori_loop(0, 2 * CHUNKS, drain, 0)


def on_device(picture_vectors, caption_vectors, sharpness_factor, affinity_offset):
    rows, depth = picture_vectors.shape
    part = rows // CHUNKS
    vmem = pl.BlockSpec(memory_space=pltpu.VMEM)
    smem = pl.BlockSpec(memory_space=pltpu.SMEM)
    anywhere = pl.BlockSpec(memory_space=pl.ANY)
    dma = pltpu.SemaphoreType.DMA
    loss, gi, gt = pl.pallas_call(
        kernel,
        name="window_loss",
        out_shape=(
            jax.ShapeDtypeStruct((1, rows), jnp.float32),
            jax.ShapeDtypeStruct((rows, depth), jnp.float32),
            jax.ShapeDtypeStruct((rows, depth), jnp.float32),
        ),
        in_specs=[smem, smem, anywhere, anywhere],
        out_specs=(vmem, vmem, vmem),
        scratch_shapes=[
            pltpu.VMEM((2, rows, depth), jnp.bfloat16),
            pltpu.VMEM((2, 2, rows, depth), jnp.bfloat16),
            pltpu.VMEM((4, 2, CHUNKS, 2 * part, depth), jnp.bfloat16),
            pltpu.VMEM((2, rows, depth), jnp.float32),
            pltpu.VMEM((rows, 2 * part), jnp.float32),
            dma((2,)),
            dma((2, CHUNKS)), dma((2, CHUNKS)),
            dma((2, 2, CHUNKS)), dma((2, 2, CHUNKS)),
            dma((2, CHUNKS)), dma((2, CHUNKS)),
            dma((4, 2, CHUNKS)), dma((4, 2, CHUNKS)),
            pltpu.SemaphoreType.REGULAR, pltpu.SemaphoreType.REGULAR,
        ],
        compiler_params=pltpu.CompilerParams(
            collective_id=0, has_side_effects=True, vmem_limit_bytes=48 * 2**20
        ),
        cost_estimate=pl.CostEstimate(
            flops=32 * 2 * rows * rows * depth, bytes_accessed=12 * rows * depth, transcendentals=32 * rows * rows
        ),
    )(sharpness_factor, affinity_offset, picture_vectors, caption_vectors)
    return loss.reshape(rows), gi, gt


def solution(mesh):
    placed = (P("dp", None), P("dp", None), P(), P())
    return jax.shard_map(
        on_device,
        mesh=mesh,
        in_specs=placed,
        out_specs=(P("dp"), P("dp", None), P("dp", None)),
        check_vma=False,
    )
```

```python
import jax
import jax.numpy as jnp
from jax import lax
from jax.experimental import pallas as pl
from jax.experimental.pallas import tpu as pltpu
from jax.sharding import PartitionSpec as P

WINDOW = 8
COLUMNS = 4
CHUNKS = 2
LANES = 384
STRIP = 32
PIECES = 4
NARROW = 16
ORDER = (
    (0, 1, 1), (1, 0, 1), (1, 1, 0), (0, 0, 0), (0, 1, 0), (0, 0, 1), (1, 0, 0), (1, 1, 1),
    (2, 0, 1), (2, 1, 0), (2, 0, 0), (2, 1, 1), (3, 0, 1), (3, 1, 0), (3, 0, 1), (3, 1, 0),
)
TEXT, IMAGE = 0, 1
OWN, CROSS = 0, 1
RIGHT, LEFT = 0, 1
MESH = pl.DeviceIdType.MESH


def window_kernel(s_ref, b_ref, img_hbm, txt_hbm, raw, hat, losses, inverses,
                  source, block, turned, in_sem, row_s, row_r, hop_s, hop_r, relay_s, relay_r, turn_s, turn_r,
                  pair_s, pair_r, row_ok, far_ok):
    rows, depth = raw.shape[1:]
    part = rows // CHUNKS
    n = lax.axis_index("dp")
    total = lax.axis_size("dp")
    core = lax.rem(n, 2)
    chip = n // 2
    column = lax.rem(chip, COLUMNS)
    row = chip // COLUMNS

    def at(offset):
        return lax.rem(n + offset + total, total)

    def in_row(offset):
        return (row * COLUMNS + lax.rem(column + offset + COLUMNS, COLUMNS)) * 2

    stride = 2 * COLUMNS
    sibling = n + 1 - 2 * core
    lead = n - core

    def lead_at(offset):
        return lax.rem(lead + offset + total, total)

    loads = [
        pltpu.make_async_copy(ref, raw.at[kind], in_sem.at[kind])
        for kind, ref in ((TEXT, txt_hbm), (IMAGE, img_hbm))
    ]
    for load in loads:
        load.start()

    barrier = pltpu.get_barrier_semaphore()

    def greet(device):
        pl.semaphore_signal(barrier, inc=1, device_id=(device,), device_id_type=MESH)

    greet(in_row(1))
    greet(in_row(-1))
    greet(lead_at(-stride))
    greet(lead_at(stride) + 1)

    @pl.when(core == 1)
    def _():
        greet(sibling)

    def rows_of(chunk):
        return pl.ds(pl.multiple_of(chunk * part, part), part)

    mine = pl.ds(0, part)
    others = pl.ds(part, part)

    def copy(src, dst, send, recv, device):
        return pltpu.make_async_remote_copy(
            src_ref=src, dst_ref=dst, send_sem=send, recv_sem=recv, device_id=(device,), device_id_type=MESH
        )

    def to_row(kind, chunk):
        target = jnp.where(kind == TEXT, at(stride), at(-stride))
        return copy(source.at[kind, OWN, rows_of(chunk)], source.at[kind, CROSS, rows_of(chunk)],
                    row_s.at[kind, chunk], row_r.at[kind, chunk], target)

    def hop(kind, way, chunk, version):
        target = jnp.where(way == RIGHT, in_row(1), in_row(-1)) + core
        return copy(source.at[kind, version, rows_of(chunk)], block.at[1 + way, kind, chunk, mine],
                    hop_s.at[way, kind, chunk], hop_r.at[way, kind, chunk], target)

    def relay(way, kind, chunk):
        return copy(block.at[1 + way, kind, chunk, mine], block.at[3, kind, chunk, mine],
                    relay_s.at[way, kind, chunk], relay_r.at[kind, chunk], beside(way))

    def beside(way):
        return jnp.where(way == RIGHT, in_row(1), in_row(-1)) + core

    ends = (column == COLUMNS - 1) | (column == 0)
    end_way = jnp.where(column == COLUMNS - 1, RIGHT, LEFT)
    end_kind = jnp.where(column == COLUMNS - 1, TEXT, IMAGE)
    upper = column >= COLUMNS // 2

    def turn(chunk):
        target = jnp.where(column == COLUMNS - 1, at(stride), at(-stride))
        return copy(block.at[1 + end_way, end_kind, chunk, mine], turned.at[chunk],
                    turn_s.at[chunk], turn_r.at[chunk], target)

    def relay_turned(chunk):
        return copy(turned.at[chunk], block.at[3, end_kind, chunk, mine],
                    relay_s.at[end_way, end_kind, chunk], relay_r.at[end_kind, chunk], beside(end_way))

    def across(group, kind, chunk, src):
        return copy(src, block.at[group, kind, chunk, others],
                    pair_s.at[group, kind, chunk], pair_r.at[group, kind, chunk], sibling)

    def sends_own(kind, way):
        first, last = column == 0, column == COLUMNS - 1
        return (
            (jnp.logical_not(last), first) if kind == TEXT else (last, jnp.logical_not(first))
        )[way]

    scale = s_ref[0]
    offset = b_ref[0]

    def normalise(kind, chunk):
        for r in range(0, part, STRIP):
            where = pl.ds(chunk * part + r, STRIP)
            full = raw[kind, where, :].astype(jnp.float32)
            inverse = 1.0 / jnp.sqrt(jnp.sum(full * full, axis=1, keepdims=True) + 1e-06)
            inverses[kind, where, :] = jnp.broadcast_to(inverse, (STRIP, 128))
            unit = (full * inverse).astype(jnp.bfloat16)
            source[kind, OWN, where, :] = unit
            block[0, kind, chunk, pl.ds(r, STRIP), :] = unit

    def own_hops(way, chunk):
        for kind in (TEXT, IMAGE):
            @pl.when(sends_own(kind, way))
            def _():
                hop(kind, way, chunk, OWN).start()

    for chunk in range(CHUNKS):
        for kind in (TEXT, IMAGE):
            if chunk == 0:
                loads[kind].wait()
            normalise(kind, chunk)
        if chunk == 0:
            @pl.when(core == 0)
            def _():
                pl.semaphore_wait(barrier, 7)
                pl.semaphore_signal(row_ok, inc=1, device_id=(sibling,), device_id_type=MESH)

            @pl.when(core == 1)
            def _():
                pl.semaphore_wait(row_ok, 1)

        if chunk == 0:
            own_hops(LEFT, 0)
        else:
            own_hops(RIGHT, 1)
        to_row(TEXT, chunk).start()

    hat[...] = jnp.zeros_like(hat)
    losses[...] = jnp.zeros_like(losses)

    @pl.when(core == 1)
    def _():
        pl.semaphore_wait(barrier, 2)
        pl.semaphore_signal(far_ok, inc=1, device_id=(sibling,), device_id_type=MESH)

    @pl.when(core == 0)
    def _():
        pl.semaphore_wait(far_ok, 1)

    for chunk in (1, 0):
        to_row(IMAGE, chunk).start()
    own_hops(RIGHT, 0)
    own_hops(LEFT, 1)

    early = (jnp.where(column == 0, IMAGE, TEXT), jnp.where(column == COLUMNS - 1, TEXT, IMAGE))
    nearer = jnp.where(upper, TEXT, IMAGE)

    def pick(step, values):
        code = 0
        for i, value in enumerate(values):
            code = code + value * (step == i).astype(jnp.int32)
        return code

    def item(step):
        stage = pick(step, [s for s, _, _ in ORDER])
        side = pick(step, [s for _, s, _ in ORDER])
        chunk = pick(step, [s for _, _, s in ORDER])
        group = jnp.where(stage == 3, 3, jnp.where(stage == 0, 0, 1 + side))
        first = jnp.where(side == 0, early[0], early[1])
        kind = jnp.where(stage == 0, side, jnp.where(stage == 1, first, 1 - first))
        kind = jnp.where(stage == 3, jnp.where(step < 14, nearer, 1 - nearer), kind)
        return stage, side, group, kind, chunk

    def arrival(step):
        stage, side, group, kind, chunk = item(step)

        for when, half in ((8, 1 - end_way), (10, end_way)):
            @pl.when(ends & (step == when))
            def _():
                turn(half).wait_recv()
                relay_turned(half).start()

        @pl.when(stage == 0)
        def _():
            to_row(kind, chunk).wait_recv()
            for way in (RIGHT, LEFT):
                owned = jnp.where(kind == TEXT, sends_own(TEXT, way), sends_own(IMAGE, way))

                @pl.when(jnp.logical_not(owned))
                def _():
                    hop(kind, way, chunk, CROSS).start()

            version = jnp.where(kind == TEXT, core, 1 - core)
            across(0, kind, chunk, source.at[kind, version, rows_of(chunk)]).start()

        @pl.when(stage > 0)
        def _():
            @pl.when(stage < 3)
            def _():
                hop(kind, side, chunk, OWN).wait_recv()

                whole = (side == RIGHT) == upper
                passes = jnp.where(whole, (kind == side).astype(jnp.int32), (chunk == 1 - side).astype(jnp.int32)) == 1
                turns = ends & (side == end_way)

                @pl.when(passes & jnp.logical_not(turns))
                def _():
                    relay(side, kind, chunk).start()

                @pl.when(passes & turns)
                def _():
                    turn(chunk).start()

            @pl.when(stage == 3)
            def _():
                relay(RIGHT, kind, chunk).wait_recv()

            across(group, kind, chunk, block.at[group, kind, chunk, mine]).start()

    def work(step):
        _, _, group, kind, chunk = item(step)
        across(group, kind, chunk, block.at[group, kind, chunk, mine]).wait_recv()
        line = lax.broadcasted_iota(jnp.int32, (rows, 2 * part), 0)
        col = lax.broadcasted_iota(jnp.int32, (rows, 2 * part), 1)
        shift = jnp.where(group == 0, chunk * part, 2 * rows)
        same = (line == col + shift) & (col < part)
        scores = lax.dot_general(
            source[1 - kind, OWN], block[group, kind, chunk], (((1,), (1,)), ((), ())),
            preferred_element_type=jnp.float32,
        )
        logits = scale * scores + offset
        logits = jnp.where(same, -logits, logits)
        small = jnp.exp(-jnp.abs(logits))
        share = 1.0 / (1.0 + small)
        sig = jnp.where(logits >= 0, share, small * share)

        @pl.when(kind == TEXT)
        def _():
            losses[...] += jnp.maximum(logits, 0.0) + jnp.log1p(small)

        slope = jnp.where(same, -sig, sig).astype(jnp.bfloat16)
        for lane in range(0, depth, LANES):
            hat[1 - kind, :, pl.ds(lane, LANES)] += jnp.dot(
                slope, block[group, kind, chunk, :, pl.ds(lane, LANES)],
                preferred_element_type=jnp.float32,
            )

    def step_body(step, carry):
        @pl.when(step < 16)
        def _():
            arrival(step)

        @pl.when(step > 0)
        def _():
            work(step - 1)

        return carry

    lax.fori_loop(0, 17, step_body, 0)

    def drain(step, carry):
        kind, chunk = step // CHUNKS, lax.rem(step, CHUNKS)
        to_row(kind, chunk).wait_send()
        for way in (RIGHT, LEFT):
            hop(kind, way, chunk, OWN).wait_send()
        for group in range(4):
            across(group, kind, chunk, block.at[group, kind, chunk, mine]).wait_send()

        return carry

    lax.fori_loop(0, 2 * CHUNKS, drain, 0)
    relay(RIGHT, TEXT, 1).wait_send()
    relay(LEFT, IMAGE, 0).wait_send()
    lower = 1 - upper.astype(jnp.int32)
    relay(RIGHT, lower, lower).wait_send()
    relay(LEFT, lower, lower).wait_send()

    @pl.when(ends)
    def _():
        for chunk in range(CHUNKS):
            turn(chunk).wait_send()


def project_kernel(s_ref, raw, hat, losses, inverses, loss_ref, gi_hbm, gt_hbm, result, sem):
    rows, depth = raw.shape[1:]
    size = rows // PIECES
    scale = s_ref[0]
    copies = []
    for kind, out in ((TEXT, gt_hbm), (IMAGE, gi_hbm)):
        for piece in range(PIECES):
            for r in range(0, size, NARROW):
                where = pl.ds(piece * size + r, NARROW)
                along = jnp.sum(raw[kind, where, :].astype(jnp.float32) * hat[kind, where, :], axis=1, keepdims=True)
                inverse = inverses[kind, where, :]
                outer = scale * inverse
                inner = outer * inverse * inverse * along
                for lane in range(0, depth, 128):
                    lanes = pl.ds(lane, 128)
                    result[kind, where, lanes] = (
                        outer * hat[kind, where, lanes] - inner * raw[kind, where, lanes].astype(jnp.float32)
                    )
            span = pl.ds(piece * size, size)
            copies.append(pltpu.make_async_copy(result.at[kind, span], out.at[span], sem.at[kind, piece]))
            copies[-1].start()
    loss_ref[...] = jnp.sum(losses[...].T, axis=0, keepdims=True) * (1.0 / (WINDOW * rows))
    for one in copies:
        one.wait()


def on_device(picture_vectors, caption_vectors, sharpness_factor, affinity_offset):
    rows, depth = picture_vectors.shape
    part = rows // CHUNKS
    vmem = pl.BlockSpec(memory_space=pltpu.VMEM)
    smem = pl.BlockSpec(memory_space=pltpu.SMEM)
    anywhere = pl.BlockSpec(memory_space=pltpu.HBM)
    dma = pltpu.SemaphoreType.DMA
    raw, hat, losses, inverses = pl.pallas_call(
        window_kernel,
        name="window_loss",
        out_shape=(
            jax.ShapeDtypeStruct((2, rows, depth), jnp.bfloat16),
            jax.ShapeDtypeStruct((2, rows, depth), jnp.float32),
            jax.ShapeDtypeStruct((rows, 2 * part), jnp.float32),
            jax.ShapeDtypeStruct((2, rows, 128), jnp.float32),
        ),
        in_specs=[smem, smem, anywhere, anywhere],
        out_specs=(vmem, vmem, vmem, vmem),
        scratch_shapes=[
            pltpu.VMEM((2, 2, rows, depth), jnp.bfloat16),
            pltpu.VMEM((4, 2, CHUNKS, 2 * part, depth), jnp.bfloat16),
            pltpu.VMEM((CHUNKS, part, depth), jnp.bfloat16),
            dma((2,)),
            dma((2, CHUNKS)), dma((2, CHUNKS)),
            dma((2, 2, CHUNKS)), dma((2, 2, CHUNKS)),
            dma((2, 2, CHUNKS)), dma((2, CHUNKS)),
            dma((CHUNKS,)), dma((CHUNKS,)),
            dma((4, 2, CHUNKS)), dma((4, 2, CHUNKS)),
            pltpu.SemaphoreType.REGULAR, pltpu.SemaphoreType.REGULAR,
        ],
        compiler_params=pltpu.CompilerParams(
            collective_id=0, has_side_effects=True, vmem_limit_bytes=48 * 2**20
        ),
        cost_estimate=pl.CostEstimate(
            flops=32 * 2 * rows * rows * depth, bytes_accessed=12 * rows * depth, transcendentals=32 * rows * rows
        ),
    )(sharpness_factor, affinity_offset, picture_vectors, caption_vectors)
    loss, gi, gt = pl.pallas_call(
        project_kernel,
        name="projection",
        out_shape=(
            jax.ShapeDtypeStruct((1, rows), jnp.float32),
            jax.ShapeDtypeStruct((rows, depth), jnp.float32),
            jax.ShapeDtypeStruct((rows, depth), jnp.float32),
        ),
        in_specs=[smem, vmem, vmem, vmem, vmem],
        out_specs=(vmem, anywhere, anywhere),
        scratch_shapes=[pltpu.VMEM((2, rows, depth), jnp.float32), dma((2, PIECES))],
        compiler_params=pltpu.CompilerParams(vmem_limit_bytes=16 * 2**20),
    )(sharpness_factor, raw, hat, losses, inverses)
    return loss.reshape(rows), gi, gt


def solution(mesh):
    placed = (P("dp", None), P("dp", None), P(), P())
    return jax.shard_map(
        on_device,
        mesh=mesh,
        in_specs=placed,
        out_specs=(P("dp"), P("dp", None), P("dp", None)),
        check_vma=False,
    )
```

```python
import jax
import jax.numpy as jnp
from jax import lax
from jax.experimental import pallas as pl
from jax.experimental.pallas import tpu as pltpu
from jax.sharding import PartitionSpec as P

WINDOW = 8
COLUMNS = 4
CHUNKS = 2
LANES = 384
STRIP = 32
PIECES = 4
NARROW = 16
LAG = 3
ORDER = (
    (0, 1, 1), (1, 0, 1), (1, 1, 0), (0, 0, 0), (0, 1, 0), (0, 0, 1), (1, 0, 0), (1, 1, 1),
    (2, 0, 1), (2, 1, 0), (2, 0, 0), (2, 1, 1), (3, 0, 1), (3, 1, 0), (3, 0, 1), (3, 1, 0),
)
TEXT, IMAGE = 0, 1
OWN, CROSS = 0, 1
RIGHT, LEFT = 0, 1
MESH = pl.DeviceIdType.MESH


def window_kernel(s_ref, b_ref, img_ref, txt_ref, hat, losses, inverses,
                  source, block, turned, row_s, row_r, hop_s, hop_r, relay_s, relay_r, turn_s, turn_r,
                  pair_s, pair_r, pair_ok, far_ok):
    rows, depth = img_ref.shape
    part = rows // CHUNKS
    n = lax.axis_index("dp")
    total = lax.axis_size("dp")
    core = lax.rem(n, 2)
    chip = n // 2
    column = lax.rem(chip, COLUMNS)
    row = chip // COLUMNS

    def at(offset):
        return lax.rem(n + offset + total, total)

    def in_row(offset):
        return (row * COLUMNS + lax.rem(column + offset + COLUMNS, COLUMNS)) * 2

    stride = 2 * COLUMNS
    sibling = n + 1 - 2 * core

    barrier = pltpu.get_barrier_semaphore()

    def greet(device):
        pl.semaphore_signal(barrier, inc=1, device_id=(device,), device_id_type=MESH)

    greet(in_row(1) + core)
    greet(in_row(-1) + core)
    greet(at(-stride))

    @pl.when(core == 1)
    def _():
        greet(sibling)

    def rows_of(chunk):
        return pl.ds(pl.multiple_of(chunk * part, part), part)

    mine = pl.ds(0, part)
    others = pl.ds(part, part)

    def copy(src, dst, send, recv, device):
        return pltpu.make_async_remote_copy(
            src_ref=src, dst_ref=dst, send_sem=send, recv_sem=recv, device_id=(device,), device_id_type=MESH
        )

    def to_row(kind, chunk):
        target = jnp.where(kind == TEXT, at(stride), at(-stride))
        return copy(source.at[kind, OWN, rows_of(chunk)], source.at[kind, CROSS, rows_of(chunk)],
                    row_s.at[kind, chunk], row_r.at[kind, chunk], target)

    def hop(kind, way, chunk, version):
        target = jnp.where(way == RIGHT, in_row(1), in_row(-1)) + core
        return copy(source.at[kind, version, rows_of(chunk)], block.at[1 + way, kind, chunk, mine],
                    hop_s.at[way, kind, chunk], hop_r.at[way, kind, chunk], target)

    def relay(way, kind, chunk):
        return copy(block.at[1 + way, kind, chunk, mine], block.at[3, kind, chunk, mine],
                    relay_s.at[way, kind, chunk], relay_r.at[kind, chunk], beside(way))

    def beside(way):
        return jnp.where(way == RIGHT, in_row(1), in_row(-1)) + core

    ends = (column == COLUMNS - 1) | (column == 0)
    end_way = jnp.where(column == COLUMNS - 1, RIGHT, LEFT)
    end_kind = jnp.where(column == COLUMNS - 1, TEXT, IMAGE)
    upper = column >= COLUMNS // 2

    def turn(chunk):
        target = jnp.where(column == COLUMNS - 1, at(stride), at(-stride))
        return copy(block.at[1 + end_way, end_kind, chunk, mine], turned.at[chunk],
                    turn_s.at[chunk], turn_r.at[chunk], target)

    def relay_turned(chunk):
        return copy(turned.at[chunk], block.at[3, end_kind, chunk, mine],
                    relay_s.at[end_way, end_kind, chunk], relay_r.at[end_kind, chunk], beside(end_way))

    def across(group, kind, chunk, src):
        return copy(src, block.at[group, kind, chunk, others],
                    pair_s.at[group, kind, chunk], pair_r.at[group, kind, chunk], sibling)

    def sends_own(kind, way):
        first, last = column == 0, column == COLUMNS - 1
        return (
            (jnp.logical_not(last), first) if kind == TEXT else (last, jnp.logical_not(first))
        )[way]

    scale = s_ref[0]
    offset = b_ref[0]

    def normalise(kind, chunk):
        for r in range(0, part, STRIP):
            where = pl.ds(chunk * part + r, STRIP)
            full = (txt_ref, img_ref)[kind][where, :].astype(jnp.float32)
            inverse = 1.0 / jnp.sqrt(jnp.sum(full * full, axis=1, keepdims=True) + 1e-06)
            inverses[kind, where, :] = jnp.broadcast_to(inverse, (STRIP, 128))
            unit = (full * inverse).astype(jnp.bfloat16)
            source[kind, OWN, where, :] = unit
            block[0, kind, chunk, pl.ds(r, STRIP), :] = unit

    def own_hops(way, chunk):
        for kind in (TEXT, IMAGE):
            @pl.when(sends_own(kind, way))
            def _():
                hop(kind, way, chunk, OWN).start()

    for chunk in range(CHUNKS):
        for kind in (TEXT, IMAGE):
            normalise(kind, chunk)
        if chunk == 0:
            @pl.when(core == 0)
            def _():
                pl.semaphore_wait(barrier, 4)
                pl.semaphore_signal(pair_ok, inc=1, device_id=(sibling,), device_id_type=MESH)

            @pl.when(core == 1)
            def _():
                pl.semaphore_wait(barrier, 3)

            pl.semaphore_signal(far_ok, inc=1, device_id=(at(stride),), device_id_type=MESH)

        if chunk == 0:
            own_hops(LEFT, 0)
        else:
            own_hops(RIGHT, 1)
        to_row(TEXT, chunk).start()

    own_hops(RIGHT, 0)
    own_hops(LEFT, 1)
    hat[...] = jnp.zeros_like(hat)
    losses[...] = jnp.zeros_like(losses)

    pl.semaphore_wait(far_ok, 1)
    for chunk in (1, 0):
        to_row(IMAGE, chunk).start()

    @pl.when(core == 1)
    def _():
        pl.semaphore_wait(pair_ok, 1)

    early = (jnp.where(column == 0, IMAGE, TEXT), jnp.where(column == COLUMNS - 1, TEXT, IMAGE))
    nearer = jnp.where(upper, TEXT, IMAGE)

    def pick(step, values):
        code = 0
        for i, value in enumerate(values):
            code = code + value * (step == i).astype(jnp.int32)
        return code

    def item(step):
        stage = pick(step, [s for s, _, _ in ORDER])
        side = pick(step, [s for _, s, _ in ORDER])
        chunk = pick(step, [s for _, _, s in ORDER])
        group = jnp.where(stage == 3, 3, jnp.where(stage == 0, 0, 1 + side))
        first = jnp.where(side == 0, early[0], early[1])
        kind = jnp.where(stage == 0, side, jnp.where(stage == 1, first, 1 - first))
        kind = jnp.where(stage == 3, jnp.where(step < 14, nearer, 1 - nearer), kind)
        return stage, side, group, kind, chunk

    def arrival(step):
        stage, side, group, kind, chunk = item(step)

        for when, half in ((8, 1 - end_way), (10, end_way)):
            @pl.when(ends & (step == when))
            def _():
                turn(half).wait_recv()
                relay_turned(half).start()

        @pl.when(stage == 0)
        def _():
            to_row(kind, chunk).wait_recv()
            for way in (RIGHT, LEFT):
                owned = jnp.where(kind == TEXT, sends_own(TEXT, way), sends_own(IMAGE, way))

                @pl.when(jnp.logical_not(owned))
                def _():
                    hop(kind, way, chunk, CROSS).start()

            version = jnp.where(kind == TEXT, core, 1 - core)
            across(0, kind, chunk, source.at[kind, version, rows_of(chunk)]).start()

        @pl.when(stage > 0)
        def _():
            @pl.when(stage < 3)
            def _():
                hop(kind, side, chunk, OWN).wait_recv()

                whole = (side == RIGHT) == upper
                passes = jnp.where(whole, (kind == side).astype(jnp.int32), (chunk == 1 - side).astype(jnp.int32)) == 1
                turns = ends & (side == end_way)

                @pl.when(passes & jnp.logical_not(turns))
                def _():
                    relay(side, kind, chunk).start()

                @pl.when(passes & turns)
                def _():
                    turn(chunk).start()

            @pl.when(stage == 3)
            def _():
                relay(RIGHT, kind, chunk).wait_recv()

            across(group, kind, chunk, block.at[group, kind, chunk, mine]).start()

    def work(step):
        _, _, group, kind, chunk = item(step)
        across(group, kind, chunk, block.at[group, kind, chunk, mine]).wait_recv()
        line = lax.broadcasted_iota(jnp.int32, (rows, 2 * part), 0)
        col = lax.broadcasted_iota(jnp.int32, (rows, 2 * part), 1)
        shift = jnp.where(group == 0, chunk * part, 2 * rows)
        same = (line == col + shift) & (col < part)
        scores = lax.dot_general(
            source[1 - kind, OWN], block[group, kind, chunk], (((1,), (1,)), ((), ())),
            preferred_element_type=jnp.float32,
        )
        logits = scale * scores + offset
        logits = jnp.where(same, -logits, logits)
        power = jnp.exp(logits)
        sig = power / (1.0 + power)

        @pl.when(kind == TEXT)
        def _():
            losses[...] += jnp.log1p(power)

        slope = jnp.where(same, -sig, sig).astype(jnp.bfloat16)
        for lane in range(0, depth, LANES):
            hat[1 - kind, :, pl.ds(lane, LANES)] += jnp.dot(
                slope, block[group, kind, chunk, :, pl.ds(lane, LANES)],
                preferred_element_type=jnp.float32,
            )

    def done(step):
        return jnp.where(step < 12, jnp.maximum(step - LAG + 1, 0), jnp.minimum(13 - LAG + 2 * (step - 12), step))

    def step_body(step, carry):
        @pl.when(step < 16)
        def _():
            arrival(step)

        lax.fori_loop(done(step - 1), done(step), lambda i, c: (work(i), c)[1], 0)
        return carry

    lax.fori_loop(0, 17, step_body, 0)

    def drain(step, carry):
        kind, chunk = step // CHUNKS, lax.rem(step, CHUNKS)
        to_row(kind, chunk).wait_send()
        for way in (RIGHT, LEFT):
            hop(kind, way, chunk, OWN).wait_send()
        for group in range(4):
            across(group, kind, chunk, block.at[group, kind, chunk, mine]).wait_send()

        return carry

    lax.fori_loop(0, 2 * CHUNKS, drain, 0)
    relay(RIGHT, TEXT, 1).wait_send()
    relay(LEFT, IMAGE, 0).wait_send()
    lower = 1 - upper.astype(jnp.int32)
    relay(RIGHT, lower, lower).wait_send()
    relay(LEFT, lower, lower).wait_send()

    @pl.when(ends)
    def _():
        for chunk in range(CHUNKS):
            turn(chunk).wait_send()


def project_kernel(s_ref, img_ref, txt_ref, hat, losses, inverses, loss_ref, gi_hbm, gt_hbm, result, sem):
    rows, depth = img_ref.shape
    size = rows // PIECES
    scale = s_ref[0]
    copies = []
    for kind, raw, out in ((TEXT, txt_ref, gt_hbm), (IMAGE, img_ref, gi_hbm)):
        for piece in range(PIECES):
            for r in range(0, size, NARROW):
                where = pl.ds(piece * size + r, NARROW)
                along = jnp.sum(raw[where, :].astype(jnp.float32) * hat[kind, where, :], axis=1, keepdims=True)
                inverse = inverses[kind, where, :]
                outer = scale * inverse
                inner = outer * inverse * inverse * along
                for lane in range(0, depth, 128):
                    lanes = pl.ds(lane, 128)
                    result[kind, where, lanes] = (
                        outer * hat[kind, where, lanes] - inner * raw[where, lanes].astype(jnp.float32)
                    )
            span = pl.ds(piece * size, size)
            copies.append(pltpu.make_async_copy(result.at[kind, span], out.at[span], sem.at[kind, piece]))
            copies[-1].start()
    loss_ref[...] = jnp.sum(losses[...].T, axis=0, keepdims=True) * (1.0 / (WINDOW * rows))
    for one in copies:
        one.wait()


def on_device(picture_vectors, caption_vectors, sharpness_factor, affinity_offset):
    rows, depth = picture_vectors.shape
    part = rows // CHUNKS
    vmem = pl.BlockSpec(memory_space=pltpu.VMEM)
    smem = pl.BlockSpec(memory_space=pltpu.SMEM)
    anywhere = pl.BlockSpec(memory_space=pltpu.HBM)
    dma = pltpu.SemaphoreType.DMA
    hat, losses, inverses = pl.pallas_call(
        window_kernel,
        name="window_loss",
        out_shape=(
            jax.ShapeDtypeStruct((2, rows, depth), jnp.float32),
            jax.ShapeDtypeStruct((rows, 2 * part), jnp.float32),
            jax.ShapeDtypeStruct((2, rows, 128), jnp.float32),
        ),
        in_specs=[smem, smem, vmem, vmem],
        out_specs=(vmem, vmem, vmem),
        scratch_shapes=[
            pltpu.VMEM((2, 2, rows, depth), jnp.bfloat16),
            pltpu.VMEM((4, 2, CHUNKS, 2 * part, depth), jnp.bfloat16),
            pltpu.VMEM((CHUNKS, part, depth), jnp.bfloat16),
            dma((2, CHUNKS)), dma((2, CHUNKS)),
            dma((2, 2, CHUNKS)), dma((2, 2, CHUNKS)),
            dma((2, 2, CHUNKS)), dma((2, CHUNKS)),
            dma((CHUNKS,)), dma((CHUNKS,)),
            dma((4, 2, CHUNKS)), dma((4, 2, CHUNKS)),
            pltpu.SemaphoreType.REGULAR, pltpu.SemaphoreType.REGULAR,
        ],
        compiler_params=pltpu.CompilerParams(
            collective_id=0, has_side_effects=True, vmem_limit_bytes=48 * 2**20
        ),
        cost_estimate=pl.CostEstimate(
            flops=32 * 2 * rows * rows * depth, bytes_accessed=12 * rows * depth, transcendentals=32 * rows * rows
        ),
    )(sharpness_factor, affinity_offset, picture_vectors, caption_vectors)
    loss, gi, gt = pl.pallas_call(
        project_kernel,
        name="projection",
        out_shape=(
            jax.ShapeDtypeStruct((1, rows), jnp.float32),
            jax.ShapeDtypeStruct((rows, depth), jnp.float32),
            jax.ShapeDtypeStruct((rows, depth), jnp.float32),
        ),
        in_specs=[smem, vmem, vmem, vmem, vmem, vmem],
        out_specs=(vmem, anywhere, anywhere),
        scratch_shapes=[pltpu.VMEM((2, rows, depth), jnp.float32), dma((2, PIECES))],
        compiler_params=pltpu.CompilerParams(vmem_limit_bytes=16 * 2**20),
    )(sharpness_factor, picture_vectors, caption_vectors, hat, losses, inverses)
    return loss.reshape(rows), gi, gt


def solution(mesh):
    placed = (P("dp", None), P("dp", None), P(), P())
    return jax.shard_map(
        on_device,
        mesh=mesh,
        in_specs=placed,
        out_specs=(P("dp"), P("dp", None), P("dp", None)),
        check_vma=False,
    )
```

```python
import jax
import jax.numpy as jnp
from jax import lax
from jax.experimental import pallas as pl
from jax.experimental.pallas import tpu as pltpu
from jax.sharding import PartitionSpec as P

WINDOW = 8
COLUMNS = 4
CHUNKS = 2
LANES = 1152
STRIP = 32
PIECES = 4
NARROW = 16
DONE = (0, 0, 0, 1, 2, 3, 4, 5, 6, 8, 9, 11, 12, 13, 14, 15, 16)
ORDER = (
    (0, 1, 1), (1, 0, 1), (1, 1, 0), (0, 0, 0), (0, 1, 0), (0, 0, 1), (1, 0, 0), (1, 1, 1),
    (2, 0, 1), (2, 1, 0), (2, 0, 0), (2, 1, 1), (3, 0, 1), (3, 1, 0), (3, 0, 1), (3, 1, 0),
)
TEXT, IMAGE = 0, 1
OWN, CROSS = 0, 1
RIGHT, LEFT = 0, 1
MESH = pl.DeviceIdType.MESH


def window_kernel(s_ref, b_ref, img_ref, txt_ref, hat, losses, inverses,
                  source, block, turned, row_s, row_r, hop_s, hop_r, relay_s, relay_r, turn_s, turn_r,
                  pair_s, pair_r, pair_ok, far_ok):
    rows, depth = img_ref.shape
    part = rows // CHUNKS
    n = lax.axis_index("dp")
    total = lax.axis_size("dp")
    core = lax.rem(n, 2)
    chip = n // 2
    column = lax.rem(chip, COLUMNS)
    row = chip // COLUMNS

    def at(offset):
        return lax.rem(n + offset + total, total)

    def in_row(offset):
        return (row * COLUMNS + lax.rem(column + offset + COLUMNS, COLUMNS)) * 2

    stride = 2 * COLUMNS
    sibling = n + 1 - 2 * core

    barrier = pltpu.get_barrier_semaphore()

    def greet(device):
        pl.semaphore_signal(barrier, inc=1, device_id=(device,), device_id_type=MESH)

    greet(in_row(1) + core)
    greet(in_row(-1) + core)
    greet(at(-stride))

    @pl.when(core == 1)
    def _():
        greet(sibling)

    def rows_of(chunk):
        return pl.ds(pl.multiple_of(chunk * part, part), part)

    mine = pl.ds(0, part)
    others = pl.ds(part, part)

    def copy(src, dst, send, recv, device):
        return pltpu.make_async_remote_copy(
            src_ref=src, dst_ref=dst, send_sem=send, recv_sem=recv, device_id=(device,), device_id_type=MESH
        )

    def to_row(kind, chunk):
        target = jnp.where(kind == TEXT, at(stride), at(-stride))
        return copy(source.at[kind, OWN, rows_of(chunk)], source.at[kind, CROSS, rows_of(chunk)],
                    row_s.at[kind, chunk], row_r.at[kind, chunk], target)

    def hop(kind, way, chunk, version):
        target = jnp.where(way == RIGHT, in_row(1), in_row(-1)) + core
        return copy(source.at[kind, version, rows_of(chunk)], block.at[1 + way, kind, chunk, mine],
                    hop_s.at[way, kind, chunk], hop_r.at[way, kind, chunk], target)

    def relay(way, kind, chunk):
        return copy(block.at[1 + way, kind, chunk, mine], block.at[3, kind, chunk, mine],
                    relay_s.at[way, kind, chunk], relay_r.at[kind, chunk], beside(way))

    def beside(way):
        return jnp.where(way == RIGHT, in_row(1), in_row(-1)) + core

    ends = (column == COLUMNS - 1) | (column == 0)
    end_way = jnp.where(column == COLUMNS - 1, RIGHT, LEFT)
    end_kind = jnp.where(column == COLUMNS - 1, TEXT, IMAGE)
    upper = column >= COLUMNS // 2

    def turn(chunk):
        target = jnp.where(column == COLUMNS - 1, at(stride), at(-stride))
        return copy(block.at[1 + end_way, end_kind, chunk, mine], turned.at[chunk],
                    turn_s.at[chunk], turn_r.at[chunk], target)

    def relay_turned(chunk):
        return copy(turned.at[chunk], block.at[3, end_kind, chunk, mine],
                    relay_s.at[end_way, end_kind, chunk], relay_r.at[end_kind, chunk], beside(end_way))

    def across(group, kind, chunk, src):
        return copy(src, block.at[group, kind, chunk, others],
                    pair_s.at[group, kind, chunk], pair_r.at[group, kind, chunk], sibling)

    def sends_own(kind, way):
        first, last = column == 0, column == COLUMNS - 1
        return (
            (jnp.logical_not(last), first) if kind == TEXT else (last, jnp.logical_not(first))
        )[way]

    scale = s_ref[0]
    offset = b_ref[0]

    def normalise(kind, chunk):
        for r in range(0, part, STRIP):
            where = pl.ds(chunk * part + r, STRIP)
            full = (txt_ref, img_ref)[kind][where, :].astype(jnp.float32)
            inverse = 1.0 / jnp.sqrt(jnp.sum(full * full, axis=1, keepdims=True) + 1e-06)
            inverses[kind, where, :] = jnp.broadcast_to(inverse, (STRIP, 128))
            unit = (full * inverse).astype(jnp.bfloat16)
            source[kind, OWN, where, :] = unit
            block[0, kind, chunk, pl.ds(r, STRIP), :] = unit

    def own_hops(way, chunk):
        for kind in (TEXT, IMAGE):
            @pl.when(sends_own(kind, way))
            def _():
                hop(kind, way, chunk, OWN).start()

    for chunk in range(CHUNKS):
        for kind in (TEXT, IMAGE):
            normalise(kind, chunk)
        if chunk == 0:
            @pl.when(core == 0)
            def _():
                pl.semaphore_wait(barrier, 4)
                pl.semaphore_signal(pair_ok, inc=1, device_id=(sibling,), device_id_type=MESH)

            @pl.when(core == 1)
            def _():
                pl.semaphore_wait(barrier, 3)

            pl.semaphore_signal(far_ok, inc=1, device_id=(at(stride),), device_id_type=MESH)

        if chunk == 0:
            own_hops(LEFT, 0)
        else:
            own_hops(RIGHT, 1)
        to_row(TEXT, chunk).start()

    own_hops(RIGHT, 0)
    own_hops(LEFT, 1)
    hat[...] = jnp.zeros_like(hat)
    losses[...] = jnp.zeros_like(losses)

    pl.semaphore_wait(far_ok, 1)
    for chunk in (1, 0):
        to_row(IMAGE, chunk).start()

    @pl.when(core == 1)
    def _():
        pl.semaphore_wait(pair_ok, 1)

    early = (jnp.where(column == 0, IMAGE, TEXT), jnp.where(column == COLUMNS - 1, TEXT, IMAGE))
    nearer = jnp.where(upper, TEXT, IMAGE)

    def pick(step, values):
        code = 0
        for i, value in enumerate(values):
            code = code + value * (step == i).astype(jnp.int32)
        return code

    def item(step):
        stage = pick(step, [s for s, _, _ in ORDER])
        side = pick(step, [s for _, s, _ in ORDER])
        chunk = pick(step, [s for _, _, s in ORDER])
        group = jnp.where(stage == 3, 3, jnp.where(stage == 0, 0, 1 + side))
        first = jnp.where(side == 0, early[0], early[1])
        kind = jnp.where(stage == 0, side, jnp.where(stage == 1, first, 1 - first))
        kind = jnp.where(stage == 3, jnp.where(step < 14, nearer, 1 - nearer), kind)
        return stage, side, group, kind, chunk

    def arrival(step):
        stage, side, group, kind, chunk = item(step)

        for when, half in ((8, 1 - end_way), (10, end_way)):
            @pl.when(ends & (step == when))
            def _():
                turn(half).wait_recv()
                relay_turned(half).start()

        @pl.when(stage == 0)
        def _():
            to_row(kind, chunk).wait_recv()
            for way in (RIGHT, LEFT):
                owned = jnp.where(kind == TEXT, sends_own(TEXT, way), sends_own(IMAGE, way))

                @pl.when(jnp.logical_not(owned))
                def _():
                    hop(kind, way, chunk, CROSS).start()

            version = jnp.where(kind == TEXT, core, 1 - core)
            across(0, kind, chunk, source.at[kind, version, rows_of(chunk)]).start()

        @pl.when(stage > 0)
        def _():
            @pl.when(stage < 3)
            def _():
                hop(kind, side, chunk, OWN).wait_recv()

                whole = (side == RIGHT) == upper
                passes = jnp.where(whole, (kind == side).astype(jnp.int32), (chunk == 1 - side).astype(jnp.int32)) == 1
                turns = ends & (side == end_way)

                @pl.when(passes & jnp.logical_not(turns))
                def _():
                    relay(side, kind, chunk).start()

                @pl.when(passes & turns)
                def _():
                    turn(chunk).start()

            @pl.when(stage == 3)
            def _():
                relay(RIGHT, kind, chunk).wait_recv()

            across(group, kind, chunk, block.at[group, kind, chunk, mine]).start()

    def work(step):
        _, _, group, kind, chunk = item(step)
        across(group, kind, chunk, block.at[group, kind, chunk, mine]).wait_recv()
        line = lax.broadcasted_iota(jnp.int32, (rows, 2 * part), 0)
        col = lax.broadcasted_iota(jnp.int32, (rows, 2 * part), 1)
        shift = jnp.where(group == 0, chunk * part, 2 * rows)
        same = (line == col + shift) & (col < part)
        scores = lax.dot_general(
            source[1 - kind, OWN], block[group, kind, chunk], (((1,), (1,)), ((), ())),
            preferred_element_type=jnp.float32,
        )
        logits = scale * scores + offset
        logits = jnp.where(same, -logits, logits)
        power = jnp.exp(logits)
        sig = power / (1.0 + power)

        @pl.when(kind == TEXT)
        def _():
            losses[...] += jnp.log1p(power)

        slope = jnp.where(same, -sig, sig).astype(jnp.bfloat16)
        for lane in range(0, depth, LANES):
            hat[1 - kind, :, pl.ds(lane, LANES)] += jnp.dot(
                slope, block[group, kind, chunk, :, pl.ds(lane, LANES)],
                preferred_element_type=jnp.float32,
            )

    def done(step):
        return pick(step, DONE)

    def step_body(step, carry):
        @pl.when(step < 16)
        def _():
            arrival(step)

        lax.fori_loop(done(step - 1), done(step), lambda i, c: (work(i), c)[1], 0)
        return carry

    lax.fori_loop(0, 17, step_body, 0)

    def drain(step, carry):
        kind, chunk = step // CHUNKS, lax.rem(step, CHUNKS)
        to_row(kind, chunk).wait_send()
        for way in (RIGHT, LEFT):
            hop(kind, way, chunk, OWN).wait_send()
        for group in range(4):
            across(group, kind, chunk, block.at[group, kind, chunk, mine]).wait_send()

        return carry

    lax.fori_loop(0, 2 * CHUNKS, drain, 0)
    relay(RIGHT, TEXT, 1).wait_send()
    relay(LEFT, IMAGE, 0).wait_send()
    lower = 1 - upper.astype(jnp.int32)
    relay(RIGHT, lower, lower).wait_send()
    relay(LEFT, lower, lower).wait_send()

    @pl.when(ends)
    def _():
        for chunk in range(CHUNKS):
            turn(chunk).wait_send()


def project_kernel(s_ref, img_ref, txt_ref, hat, losses, inverses, loss_ref, gi_hbm, gt_hbm, result, sem):
    rows, depth = img_ref.shape
    size = rows // PIECES
    scale = s_ref[0]
    copies = []
    for kind, raw, out in ((TEXT, txt_ref, gt_hbm), (IMAGE, img_ref, gi_hbm)):
        for piece in range(PIECES):
            for r in range(0, size, NARROW):
                where = pl.ds(piece * size + r, NARROW)
                along = jnp.sum(raw[where, :].astype(jnp.float32) * hat[kind, where, :], axis=1, keepdims=True)
                inverse = inverses[kind, where, :]
                outer = scale * inverse
                inner = outer * inverse * inverse * along
                for lane in range(0, depth, 128):
                    lanes = pl.ds(lane, 128)
                    result[kind, where, lanes] = (
                        outer * hat[kind, where, lanes] - inner * raw[where, lanes].astype(jnp.float32)
                    )
            span = pl.ds(piece * size, size)
            copies.append(pltpu.make_async_copy(result.at[kind, span], out.at[span], sem.at[kind, piece]))
            copies[-1].start()
    loss_ref[...] = jnp.sum(losses[...].T, axis=0, keepdims=True) * (1.0 / (WINDOW * rows))
    for one in copies:
        one.wait()


def on_device(picture_vectors, caption_vectors, sharpness_factor, affinity_offset):
    rows, depth = picture_vectors.shape
    part = rows // CHUNKS
    vmem = pl.BlockSpec(memory_space=pltpu.VMEM)
    smem = pl.BlockSpec(memory_space=pltpu.SMEM)
    anywhere = pl.BlockSpec(memory_space=pltpu.HBM)
    dma = pltpu.SemaphoreType.DMA
    hat, losses, inverses = pl.pallas_call(
        window_kernel,
        name="window_loss",
        out_shape=(
            jax.ShapeDtypeStruct((2, rows, depth), jnp.float32),
            jax.ShapeDtypeStruct((rows, 2 * part), jnp.float32),
            jax.ShapeDtypeStruct((2, rows, 128), jnp.float32),
        ),
        in_specs=[smem, smem, vmem, vmem],
        out_specs=(vmem, vmem, vmem),
        scratch_shapes=[
            pltpu.VMEM((2, 2, rows, depth), jnp.bfloat16),
            pltpu.VMEM((4, 2, CHUNKS, 2 * part, depth), jnp.bfloat16),
            pltpu.VMEM((CHUNKS, part, depth), jnp.bfloat16),
            dma((2, CHUNKS)), dma((2, CHUNKS)),
            dma((2, 2, CHUNKS)), dma((2, 2, CHUNKS)),
            dma((2, 2, CHUNKS)), dma((2, CHUNKS)),
            dma((CHUNKS,)), dma((CHUNKS,)),
            dma((4, 2, CHUNKS)), dma((4, 2, CHUNKS)),
            pltpu.SemaphoreType.REGULAR, pltpu.SemaphoreType.REGULAR,
        ],
        compiler_params=pltpu.CompilerParams(
            collective_id=0, has_side_effects=True, vmem_limit_bytes=48 * 2**20
        ),
        cost_estimate=pl.CostEstimate(
            flops=32 * 2 * rows * rows * depth, bytes_accessed=12 * rows * depth, transcendentals=32 * rows * rows
        ),
    )(sharpness_factor, affinity_offset, picture_vectors, caption_vectors)
    loss, gi, gt = pl.pallas_call(
        project_kernel,
        name="projection",
        out_shape=(
            jax.ShapeDtypeStruct((1, rows), jnp.float32),
            jax.ShapeDtypeStruct((rows, depth), jnp.float32),
            jax.ShapeDtypeStruct((rows, depth), jnp.float32),
        ),
        in_specs=[smem, vmem, vmem, vmem, vmem, vmem],
        out_specs=(vmem, anywhere, anywhere),
        scratch_shapes=[pltpu.VMEM((2, rows, depth), jnp.float32), dma((2, PIECES))],
        compiler_params=pltpu.CompilerParams(vmem_limit_bytes=16 * 2**20),
    )(sharpness_factor, picture_vectors, caption_vectors, hat, losses, inverses)
    return loss.reshape(rows), gi, gt


def solution(mesh):
    placed = (P("dp", None), P("dp", None), P(), P())
    return jax.shard_map(
        on_device,
        mesh=mesh,
        in_specs=placed,
        out_specs=(P("dp"), P("dp", None), P("dp", None)),
        check_vma=False,
    )
```

```python
import jax
import jax.numpy as jnp
from jax import lax
from jax.experimental import pallas as pl
from jax.experimental.pallas import tpu as pltpu
from jax.sharding import PartitionSpec as P

WINDOW = 8
COLUMNS = 4
CHUNKS = 2
LANES = 1152
STRIP = 32
PIECES = 4
NARROW = 16
DONE = (0, 0, 0, 1, 2, 3, 4, 5, 7, 9, 10, 11, 12, 13, 14, 15, 16)
ORDER = (
    (0, 1, 1), (1, 0, 1), (1, 1, 0), (0, 0, 0), (0, 1, 0), (0, 0, 1), (1, 0, 0), (1, 1, 1),
    (2, 0, 1), (2, 1, 0), (2, 0, 0), (2, 1, 1), (3, 0, 1), (3, 1, 0), (3, 0, 1), (3, 1, 0),
)
TEXT, IMAGE = 0, 1
OWN, CROSS = 0, 1
RIGHT, LEFT = 0, 1
MESH = pl.DeviceIdType.MESH


def window_kernel(s_ref, b_ref, img_ref, txt_ref, hat, losses, inverses,
                  source, block, turned, row_s, row_r, hop_s, hop_r, relay_s, relay_r, turn_s, turn_r,
                  pair_s, pair_r, pair_ok, far_ok):
    rows, depth = img_ref.shape
    part = rows // CHUNKS
    n = lax.axis_index("dp")
    total = lax.axis_size("dp")
    core = lax.rem(n, 2)
    chip = n // 2
    column = lax.rem(chip, COLUMNS)
    row = chip // COLUMNS

    def at(offset):
        return lax.rem(n + offset + total, total)

    def in_row(offset):
        return (row * COLUMNS + lax.rem(column + offset + COLUMNS, COLUMNS)) * 2

    stride = 2 * COLUMNS
    sibling = n + 1 - 2 * core

    barrier = pltpu.get_barrier_semaphore()

    def greet(device):
        pl.semaphore_signal(barrier, inc=1, device_id=(device,), device_id_type=MESH)

    greet(in_row(1) + core)
    greet(in_row(-1) + core)
    greet(at(-stride))

    @pl.when(core == 1)
    def _():
        greet(sibling)

    def rows_of(chunk):
        return pl.ds(pl.multiple_of(chunk * part, part), part)

    mine = pl.ds(0, part)
    others = pl.ds(part, part)

    def copy(src, dst, send, recv, device):
        return pltpu.make_async_remote_copy(
            src_ref=src, dst_ref=dst, send_sem=send, recv_sem=recv, device_id=(device,), device_id_type=MESH
        )

    def to_row(kind, chunk):
        target = jnp.where(kind == TEXT, at(stride), at(-stride))
        return copy(source.at[kind, OWN, rows_of(chunk)], source.at[kind, CROSS, rows_of(chunk)],
                    row_s.at[kind, chunk], row_r.at[kind, chunk], target)

    def hop(kind, way, chunk, version):
        target = jnp.where(way == RIGHT, in_row(1), in_row(-1)) + core
        return copy(source.at[kind, version, rows_of(chunk)], block.at[1 + way, kind, chunk, mine],
                    hop_s.at[way, kind, chunk], hop_r.at[way, kind, chunk], target)

    def relay(way, kind, chunk):
        return copy(block.at[1 + way, kind, chunk, mine], block.at[3, kind, chunk, mine],
                    relay_s.at[way, kind, chunk], relay_r.at[kind, chunk], beside(way))

    def beside(way):
        return jnp.where(way == RIGHT, in_row(1), in_row(-1)) + core

    ends = (column == COLUMNS - 1) | (column == 0)
    end_way = jnp.where(column == COLUMNS - 1, RIGHT, LEFT)
    end_kind = jnp.where(column == COLUMNS - 1, TEXT, IMAGE)
    upper = column >= COLUMNS // 2

    def turn(chunk):
        target = jnp.where(column == COLUMNS - 1, at(stride), at(-stride))
        return copy(block.at[1 + end_way, end_kind, chunk, mine], turned.at[chunk],
                    turn_s.at[chunk], turn_r.at[chunk], target)

    def relay_turned(chunk):
        return copy(turned.at[chunk], block.at[3, end_kind, chunk, mine],
                    relay_s.at[end_way, end_kind, chunk], relay_r.at[end_kind, chunk], beside(end_way))

    def across(group, kind, chunk, src):
        return copy(src, block.at[group, kind, chunk, others],
                    pair_s.at[group, kind, chunk], pair_r.at[group, kind, chunk], sibling)

    def sends_own(kind, way):
        first, last = column == 0, column == COLUMNS - 1
        return (
            (jnp.logical_not(last), first) if kind == TEXT else (last, jnp.logical_not(first))
        )[way]

    scale = s_ref[0]
    offset = b_ref[0]

    def normalise(kind, chunk):
        for r in range(0, part, STRIP):
            where = pl.ds(chunk * part + r, STRIP)
            full = (txt_ref, img_ref)[kind][where, :].astype(jnp.float32)
            inverse = 1.0 / jnp.sqrt(jnp.sum(full * full, axis=1, keepdims=True) + 1e-06)
            inverses[kind, where, :] = jnp.broadcast_to(inverse, (STRIP, 128))
            unit = (full * inverse).astype(jnp.bfloat16)
            source[kind, OWN, where, :] = unit
            block[0, kind, chunk, pl.ds(r, STRIP), :] = unit

    def own_hops(way, chunk):
        for kind in (TEXT, IMAGE):
            @pl.when(sends_own(kind, way))
            def _():
                hop(kind, way, chunk, OWN).start()

    for chunk in range(CHUNKS):
        for kind in (TEXT, IMAGE):
            normalise(kind, chunk)
        if chunk == 0:
            @pl.when(core == 0)
            def _():
                pl.semaphore_wait(barrier, 4)
                pl.semaphore_signal(pair_ok, inc=1, device_id=(sibling,), device_id_type=MESH)

            @pl.when(core == 1)
            def _():
                pl.semaphore_wait(barrier, 3)

            pl.semaphore_signal(far_ok, inc=1, device_id=(at(stride),), device_id_type=MESH)

        if chunk == 0:
            own_hops(LEFT, 0)
        else:
            own_hops(RIGHT, 1)
        to_row(TEXT, chunk).start()

    own_hops(RIGHT, 0)
    own_hops(LEFT, 1)

    pl.semaphore_wait(far_ok, 1)
    for chunk in (1, 0):
        to_row(IMAGE, chunk).start()

    @pl.when(core == 1)
    def _():
        pl.semaphore_wait(pair_ok, 1)

    hat[...] = jnp.zeros_like(hat)
    losses[...] = jnp.zeros_like(losses)

    early = (jnp.where(column == 0, IMAGE, TEXT), jnp.where(column == COLUMNS - 1, TEXT, IMAGE))
    nearer = jnp.where(upper, TEXT, IMAGE)

    def pick(step, values):
        code = 0
        for i, value in enumerate(values):
            code = code + value * (step == i).astype(jnp.int32)
        return code

    def item(step):
        stage = pick(step, [s for s, _, _ in ORDER])
        side = pick(step, [s for _, s, _ in ORDER])
        chunk = pick(step, [s for _, _, s in ORDER])
        group = jnp.where(stage == 3, 3, jnp.where(stage == 0, 0, 1 + side))
        first = jnp.where(side == 0, early[0], early[1])
        kind = jnp.where(stage == 0, side, jnp.where(stage == 1, first, 1 - first))
        kind = jnp.where(stage == 3, jnp.where(step < 14, nearer, 1 - nearer), kind)
        return stage, side, group, kind, chunk

    def arrival(step):
        stage, side, group, kind, chunk = item(step)

        for when, half in ((8, 1 - end_way), (10, end_way)):
            @pl.when(ends & (step == when))
            def _():
                turn(half).wait_recv()
                relay_turned(half).start()

        @pl.when(stage == 0)
        def _():
            to_row(kind, chunk).wait_recv()
            for way in (RIGHT, LEFT):
                owned = jnp.where(kind == TEXT, sends_own(TEXT, way), sends_own(IMAGE, way))

                @pl.when(jnp.logical_not(owned))
                def _():
                    hop(kind, way, chunk, CROSS).start()

            version = jnp.where(kind == TEXT, core, 1 - core)
            across(0, kind, chunk, source.at[kind, version, rows_of(chunk)]).start()

        @pl.when(stage > 0)
        def _():
            @pl.when(stage < 3)
            def _():
                hop(kind, side, chunk, OWN).wait_recv()

                whole = (side == RIGHT) == upper
                passes = jnp.where(whole, (kind == side).astype(jnp.int32), (chunk == 1 - side).astype(jnp.int32)) == 1
                turns = ends & (side == end_way)

                @pl.when(passes & jnp.logical_not(turns))
                def _():
                    relay(side, kind, chunk).start()

                @pl.when(passes & turns)
                def _():
                    turn(chunk).start()

            @pl.when(stage == 3)
            def _():
                relay(RIGHT, kind, chunk).wait_recv()

            across(group, kind, chunk, block.at[group, kind, chunk, mine]).start()

    def work(step):
        _, _, group, kind, chunk = item(step)
        across(group, kind, chunk, block.at[group, kind, chunk, mine]).wait_recv()
        line = lax.broadcasted_iota(jnp.int32, (rows, 2 * part), 0)
        col = lax.broadcasted_iota(jnp.int32, (rows, 2 * part), 1)
        shift = jnp.where(group == 0, chunk * part, 2 * rows)
        same = (line == col + shift) & (col < part)
        scores = lax.dot_general(
            source[1 - kind, OWN], block[group, kind, chunk], (((1,), (1,)), ((), ())),
            preferred_element_type=jnp.float32,
        )
        logits = scale * scores + offset
        logits = jnp.where(same, -logits, logits)
        power = jnp.exp(logits)
        sig = power / (1.0 + power)

        @pl.when(kind == TEXT)
        def _():
            losses[...] += jnp.log1p(power)

        slope = jnp.where(same, -sig, sig).astype(jnp.bfloat16)
        for lane in range(0, depth, LANES):
            hat[1 - kind, :, pl.ds(lane, LANES)] += jnp.dot(
                slope, block[group, kind, chunk, :, pl.ds(lane, LANES)],
                preferred_element_type=jnp.float32,
            )

    def done(step):
        return pick(step, DONE)

    def step_body(step, carry):
        @pl.when(step < 16)
        def _():
            arrival(step)

        lax.fori_loop(done(step - 1), done(step), lambda i, c: (work(i), c)[1], 0)
        return carry

    lax.fori_loop(0, 17, step_body, 0)

    def drain(step, carry):
        kind, chunk = step // CHUNKS, lax.rem(step, CHUNKS)
        to_row(kind, chunk).wait_send()
        for way in (RIGHT, LEFT):
            hop(kind, way, chunk, OWN).wait_send()
        for group in range(4):
            across(group, kind, chunk, block.at[group, kind, chunk, mine]).wait_send()

        return carry

    lax.fori_loop(0, 2 * CHUNKS, drain, 0)
    relay(RIGHT, TEXT, 1).wait_send()
    relay(LEFT, IMAGE, 0).wait_send()
    lower = 1 - upper.astype(jnp.int32)
    relay(RIGHT, lower, lower).wait_send()
    relay(LEFT, lower, lower).wait_send()

    @pl.when(ends)
    def _():
        for chunk in range(CHUNKS):
            turn(chunk).wait_send()


def project_kernel(s_ref, img_ref, txt_ref, hat, losses, inverses, loss_ref, gi_hbm, gt_hbm, result, sem):
    rows, depth = img_ref.shape
    size = rows // PIECES
    scale = s_ref[0]
    copies = []
    for kind, raw, out in ((TEXT, txt_ref, gt_hbm), (IMAGE, img_ref, gi_hbm)):
        for piece in range(PIECES):
            for r in range(0, size, NARROW):
                where = pl.ds(piece * size + r, NARROW)
                along = jnp.sum(raw[where, :].astype(jnp.float32) * hat[kind, where, :], axis=1, keepdims=True)
                inverse = inverses[kind, where, :]
                outer = scale * inverse
                inner = outer * inverse * inverse * along
                for lane in range(0, depth, 128):
                    lanes = pl.ds(lane, 128)
                    result[kind, where, lanes] = (
                        outer * hat[kind, where, lanes] - inner * raw[where, lanes].astype(jnp.float32)
                    )
            span = pl.ds(piece * size, size)
            copies.append(pltpu.make_async_copy(result.at[kind, span], out.at[span], sem.at[kind, piece]))
            copies[-1].start()
    loss_ref[...] = jnp.sum(losses[...].T, axis=0, keepdims=True) * (1.0 / (WINDOW * rows))
    for one in copies:
        one.wait()


def on_device(picture_vectors, caption_vectors, sharpness_factor, affinity_offset):
    rows, depth = picture_vectors.shape
    part = rows // CHUNKS
    vmem = pl.BlockSpec(memory_space=pltpu.VMEM)
    smem = pl.BlockSpec(memory_space=pltpu.SMEM)
    anywhere = pl.BlockSpec(memory_space=pltpu.HBM)
    dma = pltpu.SemaphoreType.DMA
    hat, losses, inverses = pl.pallas_call(
        window_kernel,
        name="window_loss",
        out_shape=(
            jax.ShapeDtypeStruct((2, rows, depth), jnp.float32),
            jax.ShapeDtypeStruct((rows, 2 * part), jnp.float32),
            jax.ShapeDtypeStruct((2, rows, 128), jnp.float32),
        ),
        in_specs=[smem, smem, vmem, vmem],
        out_specs=(vmem, vmem, vmem),
        scratch_shapes=[
            pltpu.VMEM((2, 2, rows, depth), jnp.bfloat16),
            pltpu.VMEM((4, 2, CHUNKS, 2 * part, depth), jnp.bfloat16),
            pltpu.VMEM((CHUNKS, part, depth), jnp.bfloat16),
            dma((2, CHUNKS)), dma((2, CHUNKS)),
            dma((2, 2, CHUNKS)), dma((2, 2, CHUNKS)),
            dma((2, 2, CHUNKS)), dma((2, CHUNKS)),
            dma((CHUNKS,)), dma((CHUNKS,)),
            dma((4, 2, CHUNKS)), dma((4, 2, CHUNKS)),
            pltpu.SemaphoreType.REGULAR, pltpu.SemaphoreType.REGULAR,
        ],
        compiler_params=pltpu.CompilerParams(
            collective_id=0, has_side_effects=True, vmem_limit_bytes=48 * 2**20
        ),
        cost_estimate=pl.CostEstimate(
            flops=32 * 2 * rows * rows * depth, bytes_accessed=12 * rows * depth, transcendentals=32 * rows * rows
        ),
    )(sharpness_factor, affinity_offset, picture_vectors, caption_vectors)
    loss, gi, gt = pl.pallas_call(
        project_kernel,
        name="projection",
        out_shape=(
            jax.ShapeDtypeStruct((1, rows), jnp.float32),
            jax.ShapeDtypeStruct((rows, depth), jnp.float32),
            jax.ShapeDtypeStruct((rows, depth), jnp.float32),
        ),
        in_specs=[smem, vmem, vmem, vmem, vmem, vmem],
        out_specs=(vmem, anywhere, anywhere),
        scratch_shapes=[pltpu.VMEM((2, rows, depth), jnp.float32), dma((2, PIECES))],
        compiler_params=pltpu.CompilerParams(vmem_limit_bytes=16 * 2**20),
    )(sharpness_factor, picture_vectors, caption_vectors, hat, losses, inverses)
    return loss.reshape(rows), gi, gt


def solution(mesh):
    placed = (P("dp", None), P("dp", None), P(), P())
    return jax.shard_map(
        on_device,
        mesh=mesh,
        in_specs=placed,
        out_specs=(P("dp"), P("dp", None), P("dp", None)),
        check_vma=False,
    )
```
